32 devices in a mesh: grp: 2 (over x), group: 16 (over z, y, core).
Axes of the slice: x: 2, y: 2, z: 4, core: 2. Of those that a mesh axis runs over, the one named last changes fastest.
Arguments:
- query_pre: bfloat16 [4096, 2240], P(('grp', 'group')), parts along dimension 0, may hold values from -6 to 6
- key_pre: bfloat16 [4096, 2240], P(('grp', 'group')), parts along dimension 0, may hold values from -6 to 6
- values: bfloat16 [4096, 2240], P(('grp', 'group')), parts along dimension 0, may hold values from -6 to 6
- out_grad: bfloat16 [4096, 2240], P(('grp', 'group')), parts along dimension 0, may hold values from -6 to 6
- block_frame: int32 [64], P(('grp', 'group')), parts along dimension 0, may hold values from 0 to 20
- frame_embed: bfloat16 [21, 2240], replicated, may hold values from -3 to 3
Outputs:
- attn_out: bfloat16 [4096, 2240], P(('grp', 'group')), parts along dimension 0
- query_grad: bfloat16 [4096, 2240], P(('grp', 'group')), parts along dimension 0
- key_grad: bfloat16 [4096, 2240], P(('grp', 'group')), parts along dimension 0
- value_grad: bfloat16 [4096, 2240], P(('grp', 'group')), parts along dimension 0
The draws below stay inside these ranges and needn't reach their ends.
There are 2 independent parts, one for each index of `grp`. The reference program is written for one: setup_inputs(seed, part) draws one part's arguments, and reference() takes and returns one part's arrays. A program takes and returns all parts, laid end to end along the dimension named above; an argument that names none is the same for every part. Nothing has to cross between parts.
All inputs are finite; a program needn't handle non-finite values.
Results may differ from the reference program's by a relative error of at most 0.0058.
Values sent between devices are 32-bit elements; how exact they have to be, the bound alone decides.
A program may use at most 320 MiB of HBM per device.

```python
import jax
import jax.numpy as jnp
from jax import lax

D = 2240
HEADS = 20
HD = 112
CL = 64
FRAMES = 21
TOKENS = 2048
BLOCKS = 32


def place_ends(entries, key, low, top_value):
    shape = entries.shape
    spot = [jax.random.randint(jax.random.fold_in(key, axis), (), 0, shape[axis]) for axis in range(len(shape))]
    entries = entries.at[tuple(spot)].set(low)
    longest = shape.index(max(shape))
    spot[longest] = (spot[longest] + 1) % shape[longest]
    return entries.at[tuple(spot)].set(top_value)


def shard_levels(rng, extent, cuts, low, top_value):
    factor_of = 1.0
    for axis_at, shards_of in cuts:
        heights = jax.random.uniform(jax.random.fold_in(jax.random.fold_in(rng, 6), axis_at), (shards_of,), jnp.float32, low / len(cuts), top_value / len(cuts))
        factor_of = factor_of * jnp.repeat(jnp.exp(heights), extent[axis_at] // shards_of).reshape((-1,) + (1,) * (len(extent) - 1 - axis_at))
    return factor_of


def normal_values(key, extent, scale, limit, shards=(), kind=jnp.bfloat16):
    values = scale * jax.random.normal(key, extent, jnp.float32)
    if shards:
        values = values * shard_levels(key, extent, shards, -0.22, 0.18)
    return jnp.clip(values, -limit, limit).astype(kind)


def setup_inputs(seed: int = 0, part: int = 0) -> dict:
    splits = jax.random.split(jax.random.key(seed), 7)
    part_keys = jax.random.split(jax.random.fold_in(splits[6], part), 7)
    query_pre = normal_values(part_keys[0], (TOKENS, D), 1.0, 6.0, ((0, 16),))
    key_pre = normal_values(part_keys[1], (TOKENS, D), 1.0, 6.0, ((0, 16),))
    values = normal_values(part_keys[2], (TOKENS, D), 1.0, 6.0, ((0, 16),))
    out_grad = normal_values(part_keys[3], (TOKENS, D), 1.0, 6.0, ((0, 16),))
    block_frame = place_ends(jax.random.randint(part_keys[4], (BLOCKS,), 0, FRAMES), jax.random.fold_in(part_keys[4], 1), 0, FRAMES - 1).astype(jnp.int32)
    frame_embed = normal_values(splits[5], (FRAMES, D), 0.5, 3.0)
    return {"query_pre": query_pre, "key_pre": key_pre, "values": values, "out_grad": out_grad, "block_frame": block_frame, "frame_embed": frame_embed}


score_scale = 4.0

def reference(query_pre, key_pre, values, out_grad, block_frame, frame_embed):
    n_blocks = TOKENS // CL
    frame_ids = jnp.arange(FRAMES, dtype=jnp.int32)
    onehot = (block_frame[:, None] == frame_ids[None, :]).astype(jnp.bfloat16)
    frame_shift = jnp.dot(onehot, frame_embed, preferred_element_type=jnp.float32)
    key_in = key_pre.reshape(n_blocks, CL, D).astype(jnp.float32) + frame_shift[:, None, :]
    key_act = jnp.maximum(key_in, 0.0).astype(jnp.bfloat16).reshape(n_blocks, CL, HEADS, HD)
    query_act = jnp.maximum(query_pre, 0).reshape(n_blocks, CL, HEADS, HD)
    value_rows = values.reshape(n_blocks, CL, HEADS, HD)
    grad_rows = out_grad.reshape(n_blocks, CL, HEADS, HD)
    block_ends = (jnp.arange(n_blocks, dtype=jnp.int32) + 1) * CL
    row_scale = score_scale / (HD * jnp.sqrt(block_ends.astype(jnp.float32)))
    zero_state = jnp.zeros((HEADS, HD, HD), jnp.float32)
    inputs = (query_act, key_act, value_rows, grad_rows, row_scale)

    def forward(carry_state, block):
        query_block, key_block, value_block, grad_block, factor = block
        carry_state = carry_state + jnp.einsum('thi,thj->hij', key_block.astype(jnp.float32), value_block.astype(jnp.float32))
        rounded = lax.optimization_barrier(carry_state.astype(jnp.bfloat16)).astype(jnp.float32)
        result = factor * jnp.einsum('thi,hij->thj', query_block.astype(jnp.float32), rounded)
        query_part = factor * jnp.einsum('thj,hij->thi', grad_block.astype(jnp.float32), rounded)
        return (carry_state, (result, query_part))

    def backward(carry_state, block):
        query_block, key_block, value_block, grad_block, factor = block
        carry_state = carry_state + factor * jnp.einsum('thi,thj->hij', query_block.astype(jnp.float32), grad_block.astype(jnp.float32))
        rounded = lax.optimization_barrier(carry_state.astype(jnp.bfloat16)).astype(jnp.float32)
        value_part = jnp.einsum('thi,hij->thj', key_block.astype(jnp.float32), rounded)
        key_part = jnp.einsum('thj,hij->thi', value_block.astype(jnp.float32), rounded)
        return (carry_state, (value_part, key_part))
    unused_a, (result, query_part) = lax.scan(forward, zero_state, inputs)
    unused_b, (value_part, key_part) = lax.scan(backward, zero_state, inputs, reverse=True)
    attn_out = result.reshape(TOKENS, D).astype(jnp.bfloat16)
    query_grad = jnp.where(query_pre > 0, query_part.reshape(TOKENS, D), 0.0).astype(jnp.bfloat16)
    key_grad = jnp.where(key_in.reshape(TOKENS, D) > 0, key_part.reshape(TOKENS, D), 0.0).astype(jnp.bfloat16)
    value_grad = value_part.reshape(TOKENS, D).astype(jnp.bfloat16)
    return (attn_out, query_grad, key_grad, value_grad)
```

```python
import functools

import jax
import jax.numpy as jnp
from jax import lax
from jax.experimental import pallas as pl
from jax.experimental.pallas import tpu as pltpu
from jax.sharding import PartitionSpec as P

HEADS = 20
HD = 112
CL = 64
CHUNK = 384
HALF = HD // 2

score_scale = 4.0
MESH = pl.DeviceIdType.MESH
F32 = jnp.float32
BF16 = jnp.bfloat16


def dot(a, b, dims):
    return lax.dot_general(a, b, (dims, ((), ())), preferred_element_type=F32)


def kernel(n, width, q_ref, k_ref, v_ref, g_ref, frame_ref, embed_ref,
           out_ref, qg_ref, kg_ref, vg_ref,
           act, total, first, sib_in, chip, pair_in, chain_in, chain_out,
           pair_out, prefix, sib_out, send_sem, recv_sem):
    packed = total.shape[2]
    chunks = packed // CHUNK
    me = lax.axis_index("group")
    core = lax.rem(me, 2)
    mid = lax.rem(me // 2, 2)
    outer = me // 4
    depth = n // 4
    place = outer + core * (depth - 1 - 2 * outer)
    has_prev = place > 0
    has_next = place < depth - 1
    lead = mid == core
    sibling = me + 1 - 2 * core
    partner = me + 2 - 4 * mid
    onward = lax.rem(me + 4 - 8 * core + n, n)
    back = lax.rem(me - 4 + 8 * core + n, n)
    mine = pl.ds(pl.multiple_of(HALF * mid, 8), HALF)
    other = pl.ds(pl.multiple_of(HALF * (1 - mid), 8), HALF)

    barrier = pltpu.get_barrier_semaphore()
    for peer in (sibling, partner, onward, back):
        pl.semaphore_signal(barrier, inc=1, device_id={"group": peer}, device_id_type=MESH)

    def lanes(k):
        return pl.ds(k * CHUNK, CHUNK)

    def copy(phase, k, src, dst, peer):
        return pltpu.make_async_remote_copy(
            src_ref=src, dst_ref=dst, send_sem=send_sem.at[phase, k],
            recv_sem=recv_sem.at[phase, k], device_id={"group": peer}, device_id_type=MESH)

    def sib_first(k):
        return copy(0, k, total.at[1 - core, :, lanes(k)], sib_in.at[:, lanes(k)], sibling)

    def pair_first(k):
        return copy(1, k, chip.at[other, lanes(k)], pair_in.at[:, lanes(k)], partner)

    def chain(k):
        return copy(2, k, chain_out.at[:, lanes(k)], chain_in.at[:, lanes(k)], onward)

    def pair_last(k):
        return copy(3, k, pair_out.at[:, lanes(k)], prefix.at[core, mine, lanes(k)], partner)

    def sib_last(k):
        return copy(4, k, sib_out.at[:, lanes(k)], prefix.at[core, :, lanes(k)], sibling)

    scales = []
    for b in range(2):
        tokens = (me * 2 + b + 1) * CL
        scales.append(score_scale / (HD * jnp.sqrt(jnp.full((1, HD), tokens, jnp.int32).astype(F32))))

    for kind in range(2):
        total[kind, :, packed - 128:] = jnp.zeros((HD, 128), F32)
    ids = lax.broadcasted_iota(jnp.int32, (CL, embed_ref.shape[0]), 1)
    for b in range(2):
        onehot = jnp.where(ids == frame_ref[b], 1.0, 0.0).astype(BF16)
        rows = slice(CL * b, CL * b + CL)
        for k in range(chunks):
            cols = slice(k * CHUNK, min(k * CHUNK + CHUNK, width))
            shift = dot(onehot, embed_ref[:, cols], ((1,), (0,)))
            act[rows, cols] = jnp.maximum(k_ref[rows, cols].astype(F32) + shift, 0.0).astype(BF16)

    def head_state(h):
        cols = slice(h * HD, h * HD + HD)
        key, value, grad = act[:, cols], v_ref[:, cols], g_ref[:, cols]
        query = jnp.maximum(q_ref[:, cols], 0)
        early, late = slice(0, CL), slice(CL, 2 * CL)
        tn = ((0,), (0,))
        kv0 = dot(key[early], value[early], tn)
        kv1 = dot(key[late], value[late], tn)
        first[0, :, cols] = kv0
        total[0, :, cols] = kv0 + kv1
        gr0 = scales[0] * dot(query[early], grad[early], tn)
        gr1 = scales[1] * dot(query[late], grad[late], tn)
        first[1, :, cols] = gr1
        total[1, :, cols] = gr0 + gr1

    done = [0]

    def stage_a(k):
        while done[0] < HEADS and done[0] * HD < (k + 1) * CHUNK:
            head_state(done[0])
            done[0] += 1
        if k == 0:
            pl.semaphore_wait(barrier, 4)
        sib_first(k).start()

    def stage_b(k):
        sib_first(k).wait_recv()
        chip[:, lanes(k)] = total[core, :, lanes(k)] + sib_in[:, lanes(k)]
        pair_first(k).start()

    def stage_c(k):
        @pl.when(has_prev)
        def _():
            chain(k).wait_recv()

        @pl.when(jnp.logical_not(has_prev))
        def _():
            chain_in[:, lanes(k)] = jnp.zeros((HALF, CHUNK), F32)

        pair_first(k).wait_recv()

        @pl.when(has_next)
        def _():
            chain_out[:, lanes(k)] = chain_in[:, lanes(k)] + (chip[mine, lanes(k)] + pair_in[:, lanes(k)])
            chain(k).start()

        @pl.when(lead)
        def _():
            pair_out[:, lanes(k)] = chain_in[:, lanes(k)] + chip[mine, lanes(k)]
            prefix[core, mine, lanes(k)] = chain_in[:, lanes(k)]

        @pl.when(jnp.logical_not(lead))
        def _():
            pair_out[:, lanes(k)] = chain_in[:, lanes(k)]
            prefix[core, mine, lanes(k)] = chain_in[:, lanes(k)] + pair_in[:, lanes(k)]

        pair_last(k).start()

    def stage_d(k):
        pair_last(k).wait_recv()
        sib_out[:, lanes(k)] = prefix[core, :, lanes(k)] + total[core, :, lanes(k)]
        sib_last(k).start()

    def head_out(h):
        cols = slice(h * HD, h * HD + HD)
        before, after = prefix[0, :, cols], prefix[1, :, cols]
        kv = [(before + first[0, :, cols]).astype(BF16), (before + total[0, :, cols]).astype(BF16)]
        gr = [(after + total[1, :, cols]).astype(BF16), (after + first[1, :, cols]).astype(BF16)]
        nn, nt = ((1,), (0,)), ((1,), (1,))
        for b in range(2):
            rows = slice(CL * b, CL * b + CL)
            query = jnp.maximum(q_ref[rows, cols], 0)
            key, value, grad = act[rows, cols], v_ref[rows, cols], g_ref[rows, cols]
            out_ref[rows, cols] = (scales[b] * dot(query, kv[b], nn)).astype(BF16)
            part = scales[b] * dot(grad, kv[b], nt)
            qg_ref[rows, cols] = jnp.where(query.astype(F32) > 0, part, 0.0).astype(BF16)
            vg_ref[rows, cols] = dot(key, gr[b], nn).astype(BF16)
            part = dot(value, gr[b], nt)
            kg_ref[rows, cols] = jnp.where(key.astype(F32) > 0, part, 0.0).astype(BF16)

    written = [0]

    def stage_e(k):
        sib_last(k).wait_recv()
        while written[0] < HEADS and (written[0] + 1) * HD <= (k + 1) * CHUNK:
            head_out(written[0])
            written[0] += 1

    order = []
    for k in range(chunks + 1):
        order += [(stage_a, k), (stage_b, k - 1)]
    for k in range(chunks + 4):
        order += [(stage_c, k), (stage_d, k - 2), (stage_e, k - 4)]
    for stage, k in order:
        if 0 <= k < chunks:
            stage(k)

    for k in range(chunks):
        sib_first(k).wait_send()
        pair_first(k).wait_send()
        pair_last(k).wait_send()
        sib_last(k).wait_send()

    @pl.when(has_next)
    def _():
        for k in range(chunks):
            chain(k).wait_send()


def local(query_pre, key_pre, values, out_grad, block_frame, frame_embed):
    n = lax.axis_size("group")
    rows, width = query_pre.shape
    packed = -(-width // CHUNK) * CHUNK
    chunks = packed // CHUNK
    vmem = pl.BlockSpec(memory_space=pltpu.VMEM)
    result = jax.ShapeDtypeStruct((rows, width), BF16)
    return pl.pallas_call(
        functools.partial(kernel, n, width),
        out_shape=(result,) * 4,
        in_specs=[vmem] * 4 + [pl.BlockSpec(memory_space=pltpu.SMEM), vmem],
        out_specs=(vmem,) * 4,
        scratch_shapes=[
            pltpu.VMEM((rows, width), BF16),
            pltpu.VMEM((2, HD, packed), F32),
            pltpu.VMEM((2, HD, packed), F32),
            pltpu.VMEM((HD, packed), F32),
            pltpu.VMEM((HD, packed), F32),
            pltpu.VMEM((HALF, packed), F32),
            pltpu.VMEM((HALF, packed), F32),
            pltpu.VMEM((HALF, packed), F32),
            pltpu.VMEM((HALF, packed), F32),
            pltpu.VMEM((2, HD, packed), F32),
            pltpu.VMEM((HD, packed), F32),
            pltpu.SemaphoreType.DMA((5, chunks)),
            pltpu.SemaphoreType.DMA((5, chunks)),
        ],
        compiler_params=pltpu.CompilerParams(
            collective_id=0, has_side_effects=True, vmem_limit_bytes=44 * 1024 * 1024),
    )(query_pre, key_pre, values, out_grad, block_frame, frame_embed)


def solution(mesh):
    rows = P(("grp", "group"), None)
    return jax.shard_map(
        local,
        mesh=mesh,
        in_specs=(rows, rows, rows, rows, P(("grp", "group")), P()),
        out_specs=(rows,) * 4,
        check_vma=False,
    )
```

```python
import functools

import jax
import jax.numpy as jnp
from jax import lax
from jax.experimental import pallas as pl
from jax.experimental.pallas import tpu as pltpu
from jax.sharding import PartitionSpec as P

HEADS = 20
HD = 112
CL = 64
CHUNK = 384
HALF = HD // 2

score_scale = 4.0
MESH = pl.DeviceIdType.MESH
F32 = jnp.float32
BF16 = jnp.bfloat16


def dot(a, b, dims):
    return lax.dot_general(a, b, (dims, ((), ())), preferred_element_type=F32)


def kernel(n, width, q_ref, k_ref, v_ref, g_ref, frame_ref, embed_ref,
           out_ref, qg_ref, kg_ref, vg_ref,
           act, total, first, local_sum, sib_in, chip, pair_in, chain_in, chain_out,
           pair_out, prefix, sib_out, send_sem, recv_sem):
    packed = total.shape[2]
    chunks = packed // CHUNK
    me = lax.axis_index("group")
    core = lax.rem(me, 2)
    mid = lax.rem(me // 2, 2)
    outer = me // 4
    depth = n // 4
    place = outer + core * (depth - 1 - 2 * outer)
    has_prev = place > 0
    has_next = place < depth - 1
    lead = mid == core
    sibling = me + 1 - 2 * core
    partner = me + 2 - 4 * mid
    onward = lax.rem(me + 4 - 8 * core + n, n)
    back = lax.rem(me - 4 + 8 * core + n, n)
    mine = pl.ds(pl.multiple_of(HALF * mid, 8), HALF)
    other = pl.ds(pl.multiple_of(HALF * (1 - mid), 8), HALF)

    barrier = pltpu.get_barrier_semaphore()
    for peer in (sibling, partner, onward, back):
        pl.semaphore_signal(barrier, inc=1, device_id={"group": peer}, device_id_type=MESH)

    def lanes(k):
        return pl.ds(k * CHUNK, CHUNK)

    def copy(phase, k, src, dst, peer):
        return pltpu.make_async_remote_copy(
            src_ref=src, dst_ref=dst, send_sem=send_sem.at[phase, k],
            recv_sem=recv_sem.at[phase, k], device_id={"group": peer}, device_id_type=MESH)

    def sib_first(k):
        return copy(0, k, total.at[1 - core, :, lanes(k)], sib_in.at[:, lanes(k)], sibling)

    def pair_first(k):
        return copy(1, k, chip.at[other, lanes(k)], pair_in.at[:, lanes(k)], partner)

    def chain(k):
        return copy(2, k, chain_out.at[:, lanes(k)], chain_in.at[:, lanes(k)], onward)

    def pair_last(k):
        return copy(3, k, pair_out.at[:, lanes(k)], prefix.at[core, mine, lanes(k)], partner)

    def sib_last(k):
        return copy(4, k, sib_out.at[:, lanes(k)], prefix.at[core, :, lanes(k)], sibling)

    lane = lax.broadcasted_iota(jnp.int32, (1, 2 * CL), 1)
    early = lane < CL
    tokens = jnp.where(early, me * 2 + 1, me * 2 + 2) * CL
    scale = score_scale / (HD * jnp.sqrt(tokens.astype(F32)))
    state_scales = []
    for b in range(2):
        tokens = jnp.full((1, HD), (me * 2 + b + 1) * CL, jnp.int32)
        state_scales.append(score_scale / (HD * jnp.sqrt(tokens.astype(F32))))
    masks = [early.astype(F32).astype(BF16), (lane >= CL).astype(F32).astype(BF16)]

    for kind in range(2):
        total[kind, :, packed - 128:] = jnp.zeros((HD, 128), F32)
    frames = embed_ref.shape[0]
    ids = lax.broadcasted_iota(jnp.int32, (frames, 2 * CL), 0)
    block = lax.broadcasted_iota(jnp.int32, (frames, 2 * CL), 1) < CL
    onehot = jnp.where(ids == jnp.where(block, frame_ref[0], frame_ref[1]), 1.0, 0.0).astype(BF16)
    acted = [0]

    def act_until(end):
        while acted[0] < end:
            part = slice(acted[0], min(acted[0] + CHUNK, width))
            shift = dot(embed_ref[:, part], onehot, ((0,), (0,)))
            act[part] = jnp.maximum(k_ref[part].astype(F32) + shift, 0.0).astype(BF16)
            acted[0] = part.stop

    def split(x):
        return jnp.concatenate([x * masks[0], x * masks[1]], axis=0)

    def head_state(h):
        part = slice(h * HD, h * HD + HD)
        act_until(part.stop)
        nt = ((1,), (1,))
        both = dot(split(act[part]), v_ref[part], nt)
        first[0, h] = both[:HD]
        both = both[:HD] + both[HD:]
        local_sum[0, h] = both
        total[0, :, part] = both
        both = dot(split(jnp.maximum(q_ref[part], 0)), g_ref[part], nt)
        late = state_scales[1] * both[HD:]
        first[1, h] = late
        both = state_scales[0] * both[:HD] + late
        local_sum[1, h] = both
        total[1, :, part] = both

    done = [0]

    def stage_a(k):
        while done[0] < HEADS and done[0] * HD < (k + 1) * CHUNK:
            head_state(done[0])
            done[0] += 1
        if k == 0:
            pl.semaphore_wait(barrier, 4)
        sib_first(k).start()

    def stage_b(k):
        sib_first(k).wait_recv()
        chip[:, lanes(k)] = total[core, :, lanes(k)] + sib_in[:, lanes(k)]
        pair_first(k).start()

    def stage_c(k):
        @pl.when(has_prev)
        def _():
            chain(k).wait_recv()

        @pl.when(jnp.logical_not(has_prev))
        def _():
            chain_in[:, lanes(k)] = jnp.zeros((HALF, CHUNK), F32)

        pair_first(k).wait_recv()

        @pl.when(has_next)
        def _():
            chain_out[:, lanes(k)] = chain_in[:, lanes(k)] + (chip[mine, lanes(k)] + pair_in[:, lanes(k)])
            chain(k).start()

        @pl.when(lead)
        def _():
            pair_out[:, lanes(k)] = chain_in[:, lanes(k)] + chip[mine, lanes(k)]
            prefix[core, mine, lanes(k)] = chain_in[:, lanes(k)]

        @pl.when(jnp.logical_not(lead))
        def _():
            pair_out[:, lanes(k)] = chain_in[:, lanes(k)]
            prefix[core, mine, lanes(k)] = chain_in[:, lanes(k)] + pair_in[:, lanes(k)]

        pair_last(k).start()

    def stage_d(k):
        pair_last(k).wait_recv()
        sib_out[:, lanes(k)] = prefix[core, :, lanes(k)] + total[core, :, lanes(k)]
        sib_last(k).start()

    def head_out(h):
        part = slice(h * HD, h * HD + HD)
        nn, tn = ((1,), (0,)), ((0,), (0,))
        query = jnp.maximum(q_ref[part], 0)
        key = act[part]
        before = prefix[0, :, part]
        state = jnp.concatenate([(before + first[0, h]).astype(BF16), (before + local_sum[0, h]).astype(BF16)], axis=0)
        out_ref[part] = (scale * dot(state, split(query), tn)).astype(BF16)
        both = dot(state, g_ref[part], nn)
        both = scale * jnp.where(early, both[:HD], both[HD:])
        qg_ref[part] = jnp.where(query.astype(F32) > 0, both, 0.0).astype(BF16)
        after = prefix[1, :, part]
        state = jnp.concatenate([(after + local_sum[1, h]).astype(BF16), (after + first[1, h]).astype(BF16)], axis=0)
        vg_ref[part] = dot(state, split(key), tn).astype(BF16)
        both = dot(state, v_ref[part], nn)
        both = jnp.where(early, both[:HD], both[HD:])
        kg_ref[part] = jnp.where(key.astype(F32) > 0, both, 0.0).astype(BF16)

    written = [0]

    def stage_e(k):
        sib_last(k).wait_recv()
        while written[0] < HEADS and (written[0] + 1) * HD <= (k + 1) * CHUNK:
            head_out(written[0])
            written[0] += 1

    order = []
    for k in range(chunks + 1):
        order += [(stage_a, k), (stage_b, k - 1)]
    for k in range(chunks + 4):
        order += [(stage_c, k), (stage_d, k - 2), (stage_e, k - 4)]
    for stage, k in order:
        if 0 <= k < chunks:
            stage(k)

    for k in range(chunks):
        sib_first(k).wait_send()
        pair_first(k).wait_send()
        pair_last(k).wait_send()
        sib_last(k).wait_send()

    @pl.when(has_next)
    def _():
        for k in range(chunks):
            chain(k).wait_send()


def local(query_pre, key_pre, values, out_grad, block_frame, frame_embed):
    n = lax.axis_size("group")
    rows, width = query_pre.shape
    packed = -(-width // CHUNK) * CHUNK
    chunks = packed // CHUNK
    vmem = pl.BlockSpec(memory_space=pltpu.VMEM)
    result = jax.ShapeDtypeStruct((width, rows), BF16)
    outs = pl.pallas_call(
        functools.partial(kernel, n, width),
        out_shape=(result,) * 4,
        in_specs=[vmem] * 4 + [pl.BlockSpec(memory_space=pltpu.SMEM), vmem],
        out_specs=(vmem,) * 4,
        scratch_shapes=[
            pltpu.VMEM((width, rows), BF16),
            pltpu.VMEM((2, HD, packed), F32),
            pltpu.VMEM((2, HEADS, HD, HD), F32),
            pltpu.VMEM((2, HEADS, HD, HD), F32),
            pltpu.VMEM((HD, packed), F32),
            pltpu.VMEM((HD, packed), F32),
            pltpu.VMEM((HALF, packed), F32),
            pltpu.VMEM((HALF, packed), F32),
            pltpu.VMEM((HALF, packed), F32),
            pltpu.VMEM((HALF, packed), F32),
            pltpu.VMEM((2, HD, packed), F32),
            pltpu.VMEM((HD, packed), F32),
            pltpu.SemaphoreType.DMA((5, chunks)),
            pltpu.SemaphoreType.DMA((5, chunks)),
        ],
        compiler_params=pltpu.CompilerParams(
            collective_id=0, has_side_effects=True, vmem_limit_bytes=44 * 1024 * 1024),
    )(query_pre.T, key_pre.T, values.T, out_grad.T, block_frame, frame_embed)
    return tuple(out.T for out in outs)


def solution(mesh):
    rows = P(("grp", "group"), None)
    return jax.shard_map(
        local,
        mesh=mesh,
        in_specs=(rows, rows, rows, rows, P(("grp", "group")), P()),
        out_specs=(rows,) * 4,
        check_vma=False,
    )
```

```python
import functools

import jax
import jax.numpy as jnp
from jax import lax
from jax.experimental import pallas as pl
from jax.experimental.pallas import tpu as pltpu
from jax.sharding import PartitionSpec as P

HEADS = 20
HD = 112
CL = 64
CHUNK = 384
HALF = HD // 2
PIECES = 2

score_scale = 4.0
MESH = pl.DeviceIdType.MESH
F32 = jnp.float32
BF16 = jnp.bfloat16


def dot(a, b, dims):
    return lax.dot_general(a, b, (dims, ((), ())), preferred_element_type=F32)


def kernel(n, width, q_hbm, k_hbm, v_hbm, g_hbm, frame_hbm, embed_hbm,
           out_hbm, qg_hbm, kg_hbm, vg_hbm,
           out_ref, qg_ref, kg_ref, vg_ref, store_sem,
           q_ref, k_ref, v_ref, g_ref, frame_ref, embed_ref, load_sem, small_sem, act, total, first, local_sum, sib_in, chip, pair_in, chain_in, chain_out,
           pair_out, prefix, sib_out, send_sem, recv_sem):
    packed = total.shape[2]
    chunks = packed // CHUNK
    me = lax.axis_index("group")
    core = lax.rem(me, 2)
    mid = lax.rem(me // 2, 2)
    outer = me // 4
    depth = n // 4
    place = outer + core * (depth - 1 - 2 * outer)
    has_prev = place > 0
    has_next = place < depth - 1
    lead = mid == core
    sibling = me + 1 - 2 * core
    partner = me + 2 - 4 * mid
    onward = lax.rem(me + 4 - 8 * core + n, n)
    back = lax.rem(me - 4 + 8 * core + n, n)
    mine = pl.ds(pl.multiple_of(HALF * mid, 8), HALF)
    other = pl.ds(pl.multiple_of(HALF * (1 - mid), 8), HALF)

    barrier = pltpu.get_barrier_semaphore()
    for peer in (sibling, partner, onward, back):
        pl.semaphore_signal(barrier, inc=1, device_id={"group": peer}, device_id_type=MESH)

    def load(k, which):
        src, dst = ((k_hbm, k_ref), (v_hbm, v_ref), (q_hbm, q_ref), (g_hbm, g_ref))[which]
        part = pl.ds(k * CHUNK, min(CHUNK, width - k * CHUNK))
        return pltpu.make_async_copy(src.at[part], dst.at[part], load_sem.at[which, k])

    small = [pltpu.make_async_copy(frame_hbm, frame_ref, small_sem.at[0]),
             pltpu.make_async_copy(embed_hbm, embed_ref, small_sem.at[1])]
    for one in small:
        one.start()
    for k in range(chunks):
        for which in range(4):
            load(k, which).start()

    def lanes(k):
        return pl.ds(k * CHUNK, CHUNK)

    def copy(phase, k, src, dst, peer):
        return pltpu.make_async_remote_copy(
            src_ref=src, dst_ref=dst, send_sem=send_sem.at[phase, k],
            recv_sem=recv_sem.at[phase, k], device_id={"group": peer}, device_id_type=MESH)

    def sib_first(k):
        return copy(0, k, total.at[1 - core, :, lanes(k)], sib_in.at[:, lanes(k)], sibling)

    def pair_first(k):
        return copy(1, k, chip.at[other, lanes(k)], pair_in.at[:, lanes(k)], partner)

    def chain(k):
        return copy(2, k, chain_out.at[:, lanes(k)], chain_in.at[:, lanes(k)], onward)

    def pair_last(k):
        return copy(3, k, pair_out.at[:, lanes(k)], prefix.at[core, mine, lanes(k)], partner)

    def sib_last(k):
        return copy(4, k, sib_out.at[:, lanes(k)], prefix.at[core, :, lanes(k)], sibling)

    lane = lax.broadcasted_iota(jnp.int32, (1, 2 * CL), 1)
    early = lane < CL
    tokens = jnp.where(early, me * 2 + 1, me * 2 + 2) * CL
    scale = score_scale / (HD * jnp.sqrt(tokens.astype(F32)))
    state_scales = []
    for b in range(2):
        tokens = jnp.full((1, HD), (me * 2 + b + 1) * CL, jnp.int32)
        state_scales.append(score_scale / (HD * jnp.sqrt(tokens.astype(F32))))
    masks = [early.astype(F32).astype(BF16), (lane >= CL).astype(F32).astype(BF16)]

    for kind in range(2):
        total[kind, :, packed - 128:] = jnp.zeros((HD, 128), F32)
    for one in small:
        one.wait()
    frames = embed_ref.shape[0]
    ids = lax.broadcasted_iota(jnp.int32, (frames, 2 * CL), 0)
    block = lax.broadcasted_iota(jnp.int32, (frames, 2 * CL), 1) < CL
    onehot = jnp.where(ids == jnp.where(block, frame_ref[0], frame_ref[1]), 1.0, 0.0).astype(BF16)
    acted = [0]

    def act_until(end):
        while acted[0] < end:
            part = slice(acted[0], min(acted[0] + CHUNK, width))
            for which in range(4):
                load(acted[0] // CHUNK, which).wait()
            shift = dot(embed_ref[:, part], onehot, ((0,), (0,)))
            act[part] = jnp.maximum(k_ref[part].astype(F32) + shift, 0.0).astype(BF16)
            acted[0] = part.stop

    def split(x):
        return jnp.concatenate([x * masks[0], x * masks[1]], axis=0)

    def head_state(h):
        part = slice(h * HD, h * HD + HD)
        act_until(part.stop)
        nt = ((1,), (1,))
        both = dot(split(act[part]), v_ref[part], nt)
        first[0, h] = both[:HD]
        both = both[:HD] + both[HD:]
        local_sum[0, h] = both
        total[0, :, part] = both
        both = dot(split(jnp.maximum(q_ref[part], 0)), g_ref[part], nt)
        late = state_scales[1] * both[HD:]
        first[1, h] = late
        both = state_scales[0] * both[:HD] + late
        local_sum[1, h] = both
        total[1, :, part] = both

    done = [0]

    def stage_a(k):
        while done[0] < HEADS and done[0] * HD < (k + 1) * CHUNK:
            head_state(done[0])
            done[0] += 1
        if k == 0:
            pl.semaphore_wait(barrier, 4)
        sib_first(k).start()

    def stage_b(k):
        sib_first(k).wait_recv()
        chip[:, lanes(k)] = total[core, :, lanes(k)] + sib_in[:, lanes(k)]
        pair_first(k).start()

    def stage_c(k):
        @pl.when(has_prev)
        def _():
            chain(k).wait_recv()

        @pl.when(jnp.logical_not(has_prev))
        def _():
            chain_in[:, lanes(k)] = jnp.zeros((HALF, CHUNK), F32)

        pair_first(k).wait_recv()

        @pl.when(has_next)
        def _():
            chain_out[:, lanes(k)] = chain_in[:, lanes(k)] + (chip[mine, lanes(k)] + pair_in[:, lanes(k)])
            chain(k).start()

        @pl.when(lead)
        def _():
            pair_out[:, lanes(k)] = chain_in[:, lanes(k)] + chip[mine, lanes(k)]
            prefix[core, mine, lanes(k)] = chain_in[:, lanes(k)]

        @pl.when(jnp.logical_not(lead))
        def _():
            pair_out[:, lanes(k)] = chain_in[:, lanes(k)]
            prefix[core, mine, lanes(k)] = chain_in[:, lanes(k)] + pair_in[:, lanes(k)]

        pair_last(k).start()

    def stage_d(k):
        pair_last(k).wait_recv()
        sib_out[:, lanes(k)] = prefix[core, :, lanes(k)] + total[core, :, lanes(k)]
        sib_last(k).start()

    def head_out(h):
        part = slice(h * HD, h * HD + HD)
        nn, tn = ((1,), (0,)), ((0,), (0,))
        query = jnp.maximum(q_ref[part], 0)
        key = act[part]
        before = prefix[0, :, part]
        state = jnp.concatenate([(before + first[0, h]).astype(BF16), (before + local_sum[0, h]).astype(BF16)], axis=0)
        out_ref[part] = (scale * dot(state, split(query), tn)).astype(BF16)
        both = dot(state, g_ref[part], nn)
        both = scale * jnp.where(early, both[:HD], both[HD:])
        qg_ref[part] = jnp.where(query.astype(F32) > 0, both, 0.0).astype(BF16)
        after = prefix[1, :, part]
        state = jnp.concatenate([(after + local_sum[1, h]).astype(BF16), (after + first[1, h]).astype(BF16)], axis=0)
        vg_ref[part] = dot(state, split(key), tn).astype(BF16)
        both = dot(state, v_ref[part], nn)
        both = jnp.where(early, both[:HD], both[HD:])
        kg_ref[part] = jnp.where(key.astype(F32) > 0, both, 0.0).astype(BF16)

    written = [0]

    def store(which, start, stop, k):
        src, dst = ((out_ref, out_hbm), (qg_ref, qg_hbm), (kg_ref, kg_hbm), (vg_ref, vg_hbm))[which]
        part = pl.ds(start * HD, (stop - start) * HD)
        return pltpu.make_async_copy(src.at[part], dst.at[part], store_sem.at[which, k])

    stores = []

    def stage_e(k):
        sib_last(k).wait_recv()
        begin = written[0]
        while written[0] < HEADS and (written[0] + 1) * HD <= (k + 1) * CHUNK:
            head_out(written[0])
            written[0] += 1
        for which in range(4):
            stores.append(store(which, begin, written[0], k))
            stores[-1].start()

    order = []
    for k in range(chunks + 1):
        order += [(stage_a, k), (stage_b, k - 1)]
    order += [(stage_c, k) for k in range(chunks)]
    for k in range(chunks + 1):
        order += [(stage_d, k), (stage_e, k - 1)]
    for stage, k in order:
        if 0 <= k < chunks:
            stage(k)

    for one in stores:
        one.wait()
    for k in range(chunks):
        sib_first(k).wait_send()
        pair_first(k).wait_send()
        pair_last(k).wait_send()
        sib_last(k).wait_send()

    @pl.when(has_next)
    def _():
        for k in range(chunks):
            chain(k).wait_send()


def finish(*refs):
    srcs, dsts, holds, (in_sem, out_sem) = refs[:4], refs[4:8], refs[8:12], refs[12:]
    size = srcs[0].shape[0] // PIECES
    loads, stores = [], []
    for i in range(4):
        for p in range(PIECES):
            part = pl.ds(p * size, size)
            loads.append(pltpu.make_async_copy(srcs[i].at[part], holds[i].at[part], in_sem.at[i, p]))
            stores.append(pltpu.make_async_copy(holds[i].at[part], dsts[i].at[part], out_sem.at[i, p]))
    for one in loads:
        one.start()
    for load, store in zip(loads, stores):
        load.wait()
        store.start()
    for one in stores:
        one.wait()


def local(query_pre, key_pre, values, out_grad, block_frame, frame_embed):
    n = lax.axis_size("group")
    rows, width = query_pre.shape
    packed = -(-width // CHUNK) * CHUNK
    chunks = packed // CHUNK
    hbm = pl.BlockSpec(memory_space=pltpu.HBM)
    result = jax.ShapeDtypeStruct((width, rows), BF16)
    outs = pl.pallas_call(
        functools.partial(kernel, n, width),
        out_shape=(result,) * 4,
        in_specs=[hbm] * 6,
        out_specs=(hbm,) * 4,
        scratch_shapes=[
            pltpu.VMEM((width, rows), BF16),
            pltpu.VMEM((width, rows), BF16),
            pltpu.VMEM((width, rows), BF16),
            pltpu.VMEM((width, rows), BF16),
            pltpu.SemaphoreType.DMA((4, chunks)),
            pltpu.VMEM((width, rows), BF16),
            pltpu.VMEM((width, rows), BF16),
            pltpu.VMEM((width, rows), BF16),
            pltpu.VMEM((width, rows), BF16),
            pltpu.SMEM(block_frame.shape, jnp.int32),
            pltpu.VMEM(frame_embed.shape, BF16),
            pltpu.SemaphoreType.DMA((4, chunks)),
            pltpu.SemaphoreType.DMA((2,)),
            pltpu.VMEM((width, rows), BF16),
            pltpu.VMEM((2, HD, packed), F32),
            pltpu.VMEM((2, HEADS, HD, HD), F32),
            pltpu.VMEM((2, HEADS, HD, HD), F32),
            pltpu.VMEM((HD, packed), F32),
            pltpu.VMEM((HD, packed), F32),
            pltpu.VMEM((HALF, packed), F32),
            pltpu.VMEM((HALF, packed), F32),
            pltpu.VMEM((HALF, packed), F32),
            pltpu.VMEM((HALF, packed), F32),
            pltpu.VMEM((2, HD, packed), F32),
            pltpu.VMEM((HD, packed), F32),
            pltpu.SemaphoreType.DMA((5, chunks)),
            pltpu.SemaphoreType.DMA((5, chunks)),
        ],
        compiler_params=pltpu.CompilerParams(
            collective_id=0, has_side_effects=True, vmem_limit_bytes=63 * 1024 * 1024),
    )(query_pre.T, key_pre.T, values.T, out_grad.T, block_frame, frame_embed)
    outs = pl.pallas_call(
        finish,
        out_shape=(result,) * 4,
        in_specs=[hbm] * 4,
        out_specs=(hbm,) * 4,
        scratch_shapes=[pltpu.VMEM((width, rows), BF16)] * 4 + [pltpu.SemaphoreType.DMA((4, PIECES))] * 2,
    )(*outs)
    return tuple(out.T for out in outs)


def solution(mesh):
    rows = P(("grp", "group"), None)
    return jax.shard_map(
        local,
        mesh=mesh,
        in_specs=(rows, rows, rows, rows, P(("grp", "group")), P()),
        out_specs=(rows,) * 4,
        check_vma=False,
    )
```

```python
import functools

import jax
import jax.numpy as jnp
from jax import lax
from jax.experimental import pallas as pl
from jax.experimental.pallas import tpu as pltpu
from jax.sharding import PartitionSpec as P

HEADS = 20
HD = 112
CL = 64
CHUNK = 384
HALF = HD // 2
PIECES = 2

score_scale = 4.0
MESH = pl.DeviceIdType.MESH
F32 = jnp.float32
BF16 = jnp.bfloat16


def dot(a, b, dims):
    return lax.dot_general(a, b, (dims, ((), ())), preferred_element_type=F32)


def kernel(n, width, q_hbm, k_hbm, v_hbm, g_hbm, frame_hbm, embed_hbm,
           out_hbm, qg_hbm, kg_hbm, vg_hbm,
           out_ref, qg_ref, kg_ref, vg_ref, store_sem,
           q_ref, k_ref, v_ref, g_ref, frame_ref, embed_ref, load_sem, small_sem, act, total, first, local_sum, sib_in, chip, pair_in, chain_in, chain_out,
           pair_out, prefix, sib_out, send_sem, recv_sem):
    packed = total.shape[2]
    chunks = packed // CHUNK
    me = lax.axis_index("group")
    core = lax.rem(me, 2)
    mid = lax.rem(me // 2, 2)
    outer = me // 4
    depth = n // 4
    place = outer + core * (depth - 1 - 2 * outer)
    has_prev = place > 0
    has_next = place < depth - 1
    lead = mid == core
    sibling = me + 1 - 2 * core
    partner = me + 2 - 4 * mid
    onward = lax.rem(me + 4 - 8 * core + n, n)
    back = lax.rem(me - 4 + 8 * core + n, n)
    mine = pl.ds(pl.multiple_of(HALF * mid, 8), HALF)
    other = pl.ds(pl.multiple_of(HALF * (1 - mid), 8), HALF)

    barrier = pltpu.get_barrier_semaphore()
    for peer in (sibling, partner, onward, back):
        pl.semaphore_signal(barrier, inc=1, device_id={"group": peer}, device_id_type=MESH)

    def load(k, which):
        src, dst = ((k_hbm, k_ref), (v_hbm, v_ref), (q_hbm, q_ref), (g_hbm, g_ref))[which]
        part = pl.ds(k * CHUNK, min(CHUNK, width - k * CHUNK))
        return pltpu.make_async_copy(src.at[part], dst.at[part], load_sem.at[which, k])

    small = [pltpu.make_async_copy(frame_hbm, frame_ref, small_sem.at[0]),
             pltpu.make_async_copy(embed_hbm, embed_ref, small_sem.at[1])]
    for one in small:
        one.start()
    for k in range(chunks):
        for which in range(4):
            load(k, which).start()

    def lanes(k):
        return pl.ds(k * CHUNK, CHUNK)

    def copy(phase, k, src, dst, peer):
        return pltpu.make_async_remote_copy(
            src_ref=src, dst_ref=dst, send_sem=send_sem.at[phase, k],
            recv_sem=recv_sem.at[phase, k], device_id={"group": peer}, device_id_type=MESH)

    def sib_first(k):
        return copy(0, k, total.at[1 - core, :, lanes(k)], sib_in.at[:, lanes(k)], sibling)

    def pair_first(k):
        return copy(1, k, chip.at[other, lanes(k)], pair_in.at[:, lanes(k)], partner)

    def chain(k):
        return copy(2, k, chain_out.at[:, lanes(k)], chain_in.at[:, lanes(k)], onward)

    def pair_last(k):
        return copy(3, k, pair_out.at[:, lanes(k)], prefix.at[core, mine, lanes(k)], partner)

    def sib_last(k):
        return copy(4, k, sib_out.at[:, lanes(k)], prefix.at[core, :, lanes(k)], sibling)

    lane = lax.broadcasted_iota(jnp.int32, (1, 2 * CL), 1)
    early = lane < CL
    tokens = jnp.where(early, me * 2 + 1, me * 2 + 2) * CL
    scale = score_scale / (HD * jnp.sqrt(tokens.astype(F32)))
    state_scales = []
    for b in range(2):
        tokens = jnp.full((1, HD), (me * 2 + b + 1) * CL, jnp.int32)
        state_scales.append(score_scale / (HD * jnp.sqrt(tokens.astype(F32))))
    masks = [early.astype(F32).astype(BF16), (lane >= CL).astype(F32).astype(BF16)]

    for kind in range(2):
        total[kind, :, packed - 128:] = jnp.zeros((HD, 128), F32)
    for one in small:
        one.wait()
    frames = embed_ref.shape[0]
    ids = lax.broadcasted_iota(jnp.int32, (frames, 2 * CL), 0)
    block = lax.broadcasted_iota(jnp.int32, (frames, 2 * CL), 1) < CL
    onehot = jnp.where(ids == jnp.where(block, frame_ref[0], frame_ref[1]), 1.0, 0.0).astype(BF16)
    acted = [0]

    def act_until(end):
        while acted[0] < end:
            part = slice(acted[0], min(acted[0] + CHUNK, width))
            for which in range(4):
                load(acted[0] // CHUNK, which).wait()
            shift = dot(embed_ref[:, part], onehot, ((0,), (0,)))
            act[part] = jnp.maximum(k_ref[part].astype(F32) + shift, 0.0).astype(BF16)
            acted[0] = part.stop

    def split(x):
        return jnp.concatenate([x * masks[0], x * masks[1]], axis=0)

    def head_state(h):
        part = slice(h * HD, h * HD + HD)
        act_until(part.stop)
        nt = ((1,), (1,))
        both = dot(split(act[part]), v_ref[part], nt)
        first[0, h] = both[:HD]
        both = both[:HD] + both[HD:]
        local_sum[0, h] = both
        total[0, :, part] = both
        both = dot(split(jnp.maximum(q_ref[part], 0)), g_ref[part], nt)
        late = state_scales[1] * both[HD:]
        first[1, h] = late
        both = state_scales[0] * both[:HD] + late
        local_sum[1, h] = both
        total[1, :, part] = both

    done = [0]

    def stage_a(k):
        while done[0] < HEADS and done[0] * HD < (k + 1) * CHUNK:
            head_state(done[0])
            done[0] += 1
        if k == 0:
            pl.semaphore_wait(barrier, 4)
        sib_first(k).start()

    def stage_b(k):
        sib_first(k).wait_recv()
        chip[:, lanes(k)] = total[core, :, lanes(k)] + sib_in[:, lanes(k)]
        pair_first(k).start()

    def stage_c(k):
        @pl.when(has_prev)
        def _():
            chain(k).wait_recv()

        @pl.when(jnp.logical_not(has_prev))
        def _():
            chain_in[:, lanes(k)] = jnp.zeros((HALF, CHUNK), F32)

        pair_first(k).wait_recv()

        @pl.when(has_next)
        def _():
            chain_out[:, lanes(k)] = chain_in[:, lanes(k)] + (chip[mine, lanes(k)] + pair_in[:, lanes(k)])
            chain(k).start()

        @pl.when(lead)
        def _():
            pair_out[:, lanes(k)] = chain_in[:, lanes(k)] + chip[mine, lanes(k)]
            prefix[core, mine, lanes(k)] = chain_in[:, lanes(k)]

        @pl.when(jnp.logical_not(lead))
        def _():
            pair_out[:, lanes(k)] = chain_in[:, lanes(k)]
            prefix[core, mine, lanes(k)] = chain_in[:, lanes(k)] + pair_in[:, lanes(k)]

        pair_last(k).start()

    def stage_d(k):
        pair_last(k).wait_recv()
        sib_out[:, lanes(k)] = prefix[core, :, lanes(k)] + total[core, :, lanes(k)]
        sib_last(k).start()

    def head_out(h):
        part = slice(h * HD, h * HD + HD)
        nn, tn = ((1,), (0,)), ((0,), (0,))
        query = jnp.maximum(q_ref[part], 0)
        key = act[part]
        before = prefix[0, :, part]
        state = jnp.concatenate([(before + first[0, h]).astype(BF16), (before + local_sum[0, h]).astype(BF16)], axis=0)
        out_ref[part] = (scale * dot(state, split(query), tn)).astype(BF16)
        both = dot(state, g_ref[part], nn)
        both = scale * jnp.where(early, both[:HD], both[HD:])
        qg_ref[part] = jnp.where(query.astype(F32) > 0, both, 0.0).astype(BF16)
        after = prefix[1, :, part]
        state = jnp.concatenate([(after + local_sum[1, h]).astype(BF16), (after + first[1, h]).astype(BF16)], axis=0)
        vg_ref[part] = dot(state, split(key), tn).astype(BF16)
        both = dot(state, v_ref[part], nn)
        both = jnp.where(early, both[:HD], both[HD:])
        kg_ref[part] = jnp.where(key.astype(F32) > 0, both, 0.0).astype(BF16)

    written = [0]

    def store(which, start, stop, k):
        src, dst = ((out_ref, out_hbm), (qg_ref, qg_hbm), (kg_ref, kg_hbm), (vg_ref, vg_hbm))[which]
        part = pl.ds(start * HD, (stop - start) * HD)
        return pltpu.make_async_copy(src.at[part], dst.at[part], store_sem.at[which, k])

    stores = []

    def stage_e(k):
        sib_last(k).wait_recv()
        begin = written[0]
        while written[0] < HEADS and (written[0] + 1) * HD <= (k + 1) * CHUNK:
            head_out(written[0])
            written[0] += 1
        for which in range(4):
            stores.append(store(which, begin, written[0], k))
            stores[-1].start()

    order = []
    for k in range(chunks + 2):
        order += [(stage_a, k), (stage_b, k - 2)]
    order += [(stage_c, k) for k in range(chunks)]
    for k in range(chunks + 1):
        order += [(stage_d, k), (stage_e, k - 1)]
    for stage, k in order:
        if 0 <= k < chunks:
            stage(k)

    for one in stores:
        one.wait()
    for k in range(chunks):
        sib_first(k).wait_send()
        pair_first(k).wait_send()
        pair_last(k).wait_send()
        sib_last(k).wait_send()

    @pl.when(has_next)
    def _():
        for k in range(chunks):
            chain(k).wait_send()


def finish(*refs):
    srcs, dsts, holds, (in_sem, out_sem) = refs[:4], refs[4:8], refs[8:12], refs[12:]
    size = srcs[0].shape[0] // PIECES
    loads, stores = [], []
    for i in range(4):
        for p in range(PIECES):
            part = pl.ds(p * size, size)
            loads.append(pltpu.make_async_copy(srcs[i].at[part], holds[i].at[part], in_sem.at[i, p]))
            stores.append(pltpu.make_async_copy(holds[i].at[part], dsts[i].at[part], out_sem.at[i, p]))
    for one in loads:
        one.start()
    for load, store in zip(loads, stores):
        load.wait()
        store.start()
    for one in stores:
        one.wait()


def local(query_pre, key_pre, values, out_grad, block_frame, frame_embed):
    n = lax.axis_size("group")
    rows, width = query_pre.shape
    packed = -(-width // CHUNK) * CHUNK
    chunks = packed // CHUNK
    hbm = pl.BlockSpec(memory_space=pltpu.HBM)
    result = jax.ShapeDtypeStruct((width, rows), BF16)
    outs = pl.pallas_call(
        functools.partial(kernel, n, width),
        out_shape=(result,) * 4,
        in_specs=[hbm] * 6,
        out_specs=(hbm,) * 4,
        scratch_shapes=[
            pltpu.VMEM((width, rows), BF16),
            pltpu.VMEM((width, rows), BF16),
            pltpu.VMEM((width, rows), BF16),
            pltpu.VMEM((width, rows), BF16),
            pltpu.SemaphoreType.DMA((4, chunks)),
            pltpu.VMEM((width, rows), BF16),
            pltpu.VMEM((width, rows), BF16),
            pltpu.VMEM((width, rows), BF16),
            pltpu.VMEM((width, rows), BF16),
            pltpu.SMEM(block_frame.shape, jnp.int32),
            pltpu.VMEM(frame_embed.shape, BF16),
            pltpu.SemaphoreType.DMA((4, chunks)),
            pltpu.SemaphoreType.DMA((2,)),
            pltpu.VMEM((width, rows), BF16),
            pltpu.VMEM((2, HD, packed), F32),
            pltpu.VMEM((2, HEADS, HD, HD), F32),
            pltpu.VMEM((2, HEADS, HD, HD), F32),
            pltpu.VMEM((HD, packed), F32),
            pltpu.VMEM((HD, packed), F32),
            pltpu.VMEM((HALF, packed), F32),
            pltpu.VMEM((HALF, packed), F32),
            pltpu.VMEM((HALF, packed), F32),
            pltpu.VMEM((HALF, packed), F32),
            pltpu.VMEM((2, HD, packed), F32),
            pltpu.VMEM((HD, packed), F32),
            pltpu.SemaphoreType.DMA((5, chunks)),
            pltpu.SemaphoreType.DMA((5, chunks)),
        ],
        compiler_params=pltpu.CompilerParams(
            collective_id=0, has_side_effects=True, vmem_limit_bytes=63 * 1024 * 1024),
    )(query_pre.T, key_pre.T, values.T, out_grad.T, block_frame, frame_embed)
    outs = pl.pallas_call(
        finish,
        out_shape=(result,) * 4,
        in_specs=[hbm] * 4,
        out_specs=(hbm,) * 4,
        scratch_shapes=[pltpu.VMEM((width, rows), BF16)] * 4 + [pltpu.SemaphoreType.DMA((4, PIECES))] * 2,
    )(*outs)
    return tuple(out.T for out in outs)


def solution(mesh):
    rows = P(("grp", "group"), None)
    return jax.shard_map(
        local,
        mesh=mesh,
        in_specs=(rows, rows, rows, rows, P(("grp", "group")), P()),
        out_specs=(rows,) * 4,
        check_vma=False,
    )
```
